32 devices in a mesh: row: 4 (over x, core), col: 8 (over z, y).
Axes of the slice: x: 2, y: 2, z: 4, core: 2. Of those that a mesh axis runs over, the one named last changes fastest.
Arguments:
- children: bfloat16 [20480, 10240], P('row', 'col'), may hold values from -6 to 6
- row_maps: int32 [2, 80], replicated, may hold values from 0 to 159, as said below
- col_maps: int32 [2, 80], replicated, may hold values from 0 to 159, as said below
- pairs: int32 [2048, 2], replicated, may hold values from 0 to 159, as said below
- lower_panel: bfloat16 [20480, 1024], P('row', 'col'), may hold values from -6 to 6
- upper_panel: bfloat16 [1024, 20480], P('row', 'col'), may hold values from -0.1875 to 0.1875
Outputs:
- front: float32 [20480, 20480], P('row', 'col')
The draws below stay inside these ranges and needn't reach their ends.
Inputs may be any that keep to these rules, and one draw needn't show every extreme that they name: Parent tile row r of the front's order is stored at tile row (r % 4) * 40 + r // 4. In the front's order each row of row_maps is increasing, child tile row i going to parent tile row 2 * i or 2 * i + 1. Of the 40 child tile rows b * 40 to b * 40 + 39 of one child, at most 20 map into any one stored block of tile rows a * 40 to a * 40 + 39, and in every such group of rows some block receives 20. Parent tile column r of the front's order is stored at tile column (r % 8) * 20 + r // 8. In the front's order each row of col_maps is increasing, child tile column j going to parent tile column 2 * j or 2 * j + 1. Of the 10 child tile columns b * 10 to b * 10 + 9 of one child, at most 3 map into any one stored block of tile columns a * 20 to a * 20 + 19, and in every such group some block receives 3. `pairs`: no pair is listed twice.
All inputs are finite; a program needn't handle non-finite values.
Results may differ from the reference program's by a relative error of at most 0.0003.
Values may be sent and summed in bfloat16 or wider, within the bound.
A program may use at most 320 MiB of HBM per device.

```python
import jax
import jax.numpy as jnp
from jax import lax

TILE = 128
C = 10240
K = 1024
P_SIZE = 20480
CT = 80
PT = 160
KC = 10
CRB = 40
PRB = 40
PC = 20
NPAIRS = 2048
N_ROW = 4
N_COL = 8


def cyclic_law(key, per_block, classes, devices, per_device):
    tile_ids = jnp.arange(CT, dtype=jnp.int32)
    block = tile_ids // per_block
    within = tile_ids % per_block
    bits = jax.random.randint(jax.random.fold_in(key, 1), (CT,), 0, 2, dtype=jnp.int32)
    common = jax.random.randint(jax.random.fold_in(key, 2), (CT,), 0, 2, dtype=jnp.int32)
    chosen = jnp.where(within % classes == 0, common[block], bits)
    logical = 2 * tile_ids + chosen
    return (logical % devices * per_device + logical // devices).astype(jnp.int32)


def draw_row_maps(key, part):
    return jnp.stack([cyclic_law(jax.random.fold_in(key, 21 + child_id), CRB, N_ROW // 2, N_ROW, PRB) for child_id in range(2)])


def draw_col_maps(key, part):
    return jnp.stack([cyclic_law(jax.random.fold_in(key, 31 + child_id), KC, N_COL // 2, N_COL, PC) for child_id in range(2)])


def draw_pairs(key, part):
    total = PT * PT
    cells = jnp.arange(total, dtype=jnp.int32)
    device = cells // PT // PRB * N_COL + cells % PT // PC
    hot_count = max(1, NPAIRS // (3 * PRB * PC))
    ranking = jax.random.permutation(jax.random.fold_in(key, 3), N_ROW * N_COL).astype(jnp.int32)
    hotter = (ranking[device] < hot_count).astype(jnp.int32)
    scores = jax.random.randint(jax.random.fold_in(key, 4), (total,), 0, 32768, dtype=jnp.int32) * total + cells + hotter * 1073741824
    unused, chosen = lax.top_k(scores, NPAIRS)
    chosen = chosen.astype(jnp.int32)
    return jnp.stack([chosen // PT, chosen % PT], axis=1).astype(jnp.int32)


def block_levels(own_key, extent, cuts, least, top_value):
    level = 1.0
    for dim, blocks in cuts:
        heights = jax.random.uniform(jax.random.fold_in(jax.random.fold_in(own_key, 6), dim), (blocks,), jnp.float32, least / len(cuts), top_value / len(cuts))
        level = level * jnp.repeat(jnp.exp(heights), extent[dim] // blocks).reshape((-1,) + (1,) * (len(extent) - 1 - dim))
    return level


def bell_draw(stream_key, dims, scale, limit, shards=(), kind=jnp.bfloat16):
    array = jax.random.normal(stream_key, dims, jnp.float32) * scale
    if len(shards) > 0:
        array = block_levels(stream_key, dims, shards, -0.22, 0.18) * array
    return jnp.clip(array, min=-limit, max=limit).astype(kind)


def setup_inputs(seed: int = 0) -> dict:
    key_of = jax.random.split(jax.random.key(seed), 7)
    return {
        "children": bell_draw(key_of[0], (2 * C, C), 1.0, 6.0, ((0, 4), (1, 8))),
        "row_maps": draw_row_maps(jax.random.fold_in(key_of[6], 71), 0),
        "col_maps": draw_col_maps(jax.random.fold_in(key_of[6], 71), 0),
        "pairs": draw_pairs(jax.random.fold_in(key_of[6], 71), 0),
        "lower_panel": bell_draw(key_of[4], (P_SIZE, K), 1.0, 6.0, ((0, 4), (1, 8))),
        "upper_panel": bell_draw(key_of[5], (K, P_SIZE), K ** -0.5, 0.1875, ((0, 4), (1, 8))),
    }


def reference(children, row_maps, col_maps, pairs, lower_panel, upper_panel):
    tile_count = C // TILE
    parent_count = 2 * tile_count
    front_tiles = jnp.zeros((parent_count, TILE, parent_count, TILE), jnp.float32)
    for child_id in range(2):
        child_block = children[child_id * C:(child_id + 1) * C].astype(jnp.float32)
        child_block = child_block.reshape(tile_count, TILE, tile_count, TILE).transpose(0, 2, 1, 3)
        front_tiles = front_tiles.at[row_maps[child_id][:, None], :, col_maps[child_id][None, :], :].add(child_block)
    lower_tiles = lower_panel.astype(jnp.float32).reshape(parent_count, TILE, K)
    upper_tiles = upper_panel.astype(jnp.float32).reshape(K, parent_count, TILE).transpose(1, 0, 2)
    groups = pairs.reshape(NPAIRS // 32, 32, 2)

    def product(pair_group):
        return jnp.einsum("nik,nkj->nij", lower_tiles[pair_group[:, 0]], upper_tiles[pair_group[:, 1]], precision=lax.Precision.HIGHEST)

    updates = lax.map(product, groups).reshape(NPAIRS, TILE, TILE)
    front_tiles = front_tiles.at[pairs[:, 0], :, pairs[:, 1], :].add(-updates)
    return front_tiles.reshape(parent_count * TILE, parent_count * TILE)
```

```python
import functools

import jax
import jax.numpy as jnp
from jax import lax
from jax.experimental import pallas as pl
from jax.experimental.pallas import tpu as pltpu
from jax.sharding import PartitionSpec as P

TILE = 128
WINDOW = 3
MESH = pl.DeviceIdType.MESH


def lanes(index):
    return pl.ds(pl.multiple_of(index * TILE, TILE), TILE)


def exchange_kernel(
    nx, nq, kc, pc,
    kids, low, up,
    recv, low_all, up_all,
    send1, recv1, send2, recv2, send3, recv3,
    up_s1, up_r1, up_s3, up_r3,
    low_sr, low_sl, low_r1, low_s2, low_r2,
):
    row = lax.axis_index("row")
    col = lax.axis_index("col")
    x, core = row // 2, row % 2
    q, p = col // 2, col % 2
    core_mate = (2 * x + 1 - core, col)
    p_mate = (row, 2 * q + 1 - p)

    barrier = pltpu.get_barrier_semaphore()
    for dx in range(nx):
        for dq in range(nq):
            if dx == 0 and dq == 0:
                continue
            pl.semaphore_signal(
                barrier, inc=1,
                device_id=(2 * lax.rem(x + dx, nx) + core, 2 * lax.rem(q + dq, nq) + p),
                device_id_type=MESH,
            )
    pl.semaphore_signal(barrier, inc=1, device_id=core_mate, device_id_type=MESH)
    pl.semaphore_signal(barrier, inc=1, device_id=p_mate, device_id_type=MESH)
    pl.semaphore_wait(barrier, nx * nq + 1)

    def remote(src, dst, ssem, rsem, device):
        return pltpu.make_async_remote_copy(
            src_ref=src, dst_ref=dst, send_sem=ssem, recv_sem=rsem,
            device_id=device, device_id_type=MESH,
        )

    def column_of(step, source_q):
        return lax.rem(step + source_q, kc)

    def unit1(step, tx):
        kk = column_of(step, q)
        j = col * kc + kk
        tq, s = j % nq, j // nq
        src = kids.at[:, tx, :, lanes(kk)]
        dst = recv.at[row, :, :, lanes(s)]
        here = (tx == x) & (tq == q)

        def far():
            device = (2 * tx + core, 2 * tq + p)
            return remote(src, dst, send1.at[kk, tx], recv1.at[x, s], device)

        def near():
            return pltpu.make_async_copy(src, dst, recv1.at[x, s])

        return here, far, near

    def issue(step):
        def one(dx, carry):
            here, far, near = unit1(step, lax.rem(x + 1 + dx, nx))

            @pl.when(here)
            def _():
                near().start()

            @pl.when(jnp.logical_not(here))
            def _():
                far().start()

            return carry

        lax.fori_loop(0, nx, one, 0)

    def drain(step):
        def one(dx, carry):
            here, far, _ = unit1(step, lax.rem(x + 1 + dx, nx))

            @pl.when(jnp.logical_not(here))
            def _():
                far().wait_send()

            return carry

        lax.fori_loop(0, nx, one, 0)

    def slot(xs, s, c):
        return recv.at[2 * xs + c, :, :, lanes(s)]

    def pair_copy(xs, s):
        ref = slot(xs, s, core)
        return remote(ref, ref, send2.at[xs, s], recv2.at[xs, s], p_mate)

    def core_copy(xs, s):
        ref = slot(xs, s, core)
        return remote(ref, ref, send3.at[xs, s], recv3.at[xs, s], core_mate)

    def arrivals(step, side, handle):
        def by_q(dq, carry):
            qs = lax.rem(q + dq, nq)
            j = (2 * qs + side) * kc + column_of(step, qs)

            @pl.when(j % nq == q)
            def _():
                lax.fori_loop(0, nx, lambda xs, c: (handle(xs, j // nq), c)[1], 0)

            return carry

        lax.fori_loop(0, nq, by_q, 0)

    def from_source(xs, s):
        ref = slot(xs, s, core)
        pltpu.make_async_copy(ref, ref, recv1.at[xs, s]).wait()
        pair_copy(xs, s).start()
        core_copy(xs, s).start()

    def from_pair(xs, s):
        pair_copy(xs, s).wait_recv()
        core_copy(xs, s).start()

    def up_far(tx):
        return remote(up, up_all.at[row], up_s1.at[tx], up_r1.at[x], (2 * tx + core, col))

    def up_core(xs):
        ref = up_all.at[2 * xs + core]
        return remote(ref, ref, up_s3.at[xs], up_r3.at[xs], core_mate)

    def low_slot(qs, side):
        if len(low_all.shape) == 3:
            return low_all.at[2 * qs + side]
        return low_all.at[:, lanes(2 * qs + side)]

    def low_step(qs, sems, to):
        ref = low_slot(qs, p)
        return remote(ref, ref, sems.at[qs], low_r1.at[qs], (row, 2 * to + p))

    def low_pair(qs):
        ref = low_slot(qs, p)
        return remote(ref, ref, low_s2.at[qs], low_r2.at[qs], p_mate)

    def goes_right(qs):
        return (qs <= q) & (q + 1 < nq)

    def goes_left(qs):
        return (qs >= q) & (q > 0)

    def low_arrived(qs):
        ref = low_slot(qs, p)
        pltpu.make_async_copy(ref, ref, low_r1.at[qs]).wait()

        @pl.when(goes_right(qs))
        def _():
            low_step(qs, low_sr, q + 1).start()

        @pl.when(goes_left(qs))
        def _():
            low_step(qs, low_sl, q - 1).start()

        low_pair(qs).start()

    def up_arrived(xs):
        ref = up_all.at[2 * xs + core]
        pltpu.make_async_copy(ref, ref, up_r1.at[xs]).wait()
        up_core(xs).start()

    pltpu.make_async_copy(low, low_slot(q, p), low_r1.at[q]).start()
    pltpu.make_async_copy(up, up_all.at[row], up_r1.at[x]).start()
    for dx in range(1, nx):
        up_far(lax.rem(x + dx, nx)).start()
    for step in range(min(WINDOW, kc)):
        issue(step)

    def main(m, carry):
        @pl.when(m < nx)
        def _():
            up_arrived(lax.rem(x + m, nx))

        @pl.when((m < nq) & (q - m >= 0))
        def _():
            low_arrived(q - m)

        @pl.when((m > 0) & (q + m < nq))
        def _():
            low_arrived(q + m)

        @pl.when(m < kc)
        def _():
            drain(m)

            @pl.when(m + WINDOW < kc)
            def _():
                issue(m + WINDOW)

            arrivals(m, p, from_source)

        @pl.when((m >= 1) & (m < kc + 1))
        def _():
            arrivals(m - 1, 1 - p, from_pair)

        return carry

    lax.fori_loop(0, max(kc + 1, nq, nx), main, 0)

    def finish_x(xs, carry):
        up_core(xs).wait()

        @pl.when(xs != x)
        def _():
            up_far(xs).wait_send()

        def finish_s(s, inner):
            j = s * nq + q

            @pl.when((j // kc) % 2 == p)
            def _():
                pair_copy(xs, s).wait_send()

            core_copy(xs, s).wait()
            return inner

        lax.fori_loop(0, pc, finish_s, 0)
        return carry

    lax.fori_loop(0, nx, finish_x, 0)

    def finish_q(qs, carry):
        low_pair(qs).wait()

        @pl.when(goes_right(qs))
        def _():
            low_step(qs, low_sr, q + 1).wait_send()

        @pl.when(goes_left(qs))
        def _():
            low_step(qs, low_sl, q - 1).wait_send()

        return carry

    lax.fori_loop(0, nq, finish_q, 0)


def exchange(children, lower_panel, upper_panel, n_row, n_col, pc):
    nx, nq = n_row // 2, n_col // 2
    rows, cols = children.shape
    kc = cols // TILE
    tk = rows // TILE // nx
    kids = children.reshape(tk, nx, TILE, cols)
    low_rows, low_cols = lower_panel.shape
    if low_cols == TILE:
        low_shape = (low_rows, n_col * TILE)
    else:
        low_shape = (n_col, low_rows, low_cols)
    dma = pltpu.SemaphoreType.DMA
    anywhere = pl.BlockSpec(memory_space=pl.ANY)
    recv, low_all, up_all = pl.pallas_call(
        functools.partial(exchange_kernel, nx, nq, kc, pc),
        out_shape=[
            jax.ShapeDtypeStruct((n_row, tk, TILE, pc * TILE), children.dtype),
            jax.ShapeDtypeStruct(low_shape, lower_panel.dtype),
            jax.ShapeDtypeStruct((n_row,) + upper_panel.shape, upper_panel.dtype),
        ],
        in_specs=[anywhere] * 3,
        out_specs=[anywhere] * 3,
        scratch_shapes=[
            dma((kc, nx)), dma((nx, pc)), dma((nx, pc)), dma((nx, pc)), dma((nx, pc)), dma((nx, pc)),
            dma((nx,)), dma((nx,)), dma((nx,)), dma((nx,)),
            dma((nq,)), dma((nq,)), dma((nq,)), dma((nq,)), dma((nq,)),
        ],
        compiler_params=pltpu.CompilerParams(
            collective_id=0, has_side_effects=True, vmem_limit_bytes=4 * 1024 * 1024
        ),
    )(kids, lower_panel, upper_panel)
    if low_cols != TILE:
        low_all = low_all.transpose(1, 0, 2).reshape(low_rows, n_col * low_cols)
    return (
        recv.reshape(2, n_row * tk * TILE // 2, pc * TILE),
        low_all,
        up_all.reshape(-1, pc * TILE),
    )


def front_kernel(band, width, masks, kids, low, up, out):
    first = pl.program_id(0) * band
    for start in range(0, out.shape[1], width):
        cols = pl.ds(start, width)
        product = jnp.dot(low[...], up[:, cols], preferred_element_type=jnp.float32)
        for k in range(band):
            rows = pl.ds(k * TILE, TILE)
            total = kids[0, rows, cols].astype(jnp.float32) * masks[0, pl.ds(first + k, 1), cols]
            total += kids[1, rows, cols].astype(jnp.float32) * masks[1, pl.ds(first + k, 1), cols]
            total -= product[k * TILE:(k + 1) * TILE] * masks[2, pl.ds(first + k, 1), cols]
            out[rows, cols] = total


def build_front(masks, kids, low, up, pr, pc):
    band = next(b for b in (4, 2, 1) if pr % b == 0)
    ncols, depth = pc * TILE, low.shape[1]
    width = next(w for w in (1280, 640, 512, 256, 128) if ncols % w == 0)
    return pl.pallas_call(
        functools.partial(front_kernel, band, width),
        grid=(pr // band,),
        out_shape=jax.ShapeDtypeStruct((pr * TILE, ncols), jnp.float32),
        in_specs=[
            pl.BlockSpec(memory_space=pltpu.VMEM),
            pl.BlockSpec((2, band * TILE, ncols), lambda i: (0, i, 0)),
            pl.BlockSpec((band * TILE, depth), lambda i: (i, 0)),
            pl.BlockSpec(memory_space=pltpu.VMEM),
        ],
        out_specs=pl.BlockSpec((band * TILE, ncols), lambda i: (i, 0)),
        compiler_params=pltpu.CompilerParams(vmem_limit_bytes=56 * 1024 * 1024),
        cost_estimate=pl.CostEstimate(
            flops=2 * pr * TILE * ncols * depth,
            bytes_accessed=8 * pr * TILE * ncols,
            transcendentals=0,
        ),
    )(masks, kids, low, up)


def body(children, row_maps, col_maps, pairs, lower_panel, upper_panel):
    n_row, n_col = lax.axis_size("row"), lax.axis_size("col")
    row, col = lax.axis_index("row"), lax.axis_index("col")
    nx, nq = n_row // 2, n_col // 2
    pr = lower_panel.shape[0] // TILE
    pc = upper_panel.shape[1] // TILE
    row_ids = row * pr + jnp.arange(pr, dtype=jnp.int32)
    col_ids = col * pc + jnp.arange(pc, dtype=jnp.int32)
    mine_rows = lax.dynamic_index_in_dim(row_maps.reshape(2, pr, nx), row // 2, 2, keepdims=False)
    mine_cols = lax.dynamic_index_in_dim(col_maps.reshape(2, pc, nq), col // 2, 2, keepdims=False)
    row_on = (mine_rows == row_ids[None]).astype(jnp.float32)
    col_on = (mine_cols == col_ids[None]).astype(jnp.float32)
    row_hit = (pairs[:, 0][:, None] == row_ids[None]).astype(jnp.bfloat16)
    col_hit = (pairs[:, 1][:, None] == col_ids[None]).astype(jnp.bfloat16)
    listed = jnp.dot(row_hit.T, col_hit, preferred_element_type=jnp.float32)
    masks = jnp.concatenate([row_on[:, :, None] * col_on[:, None, :], listed[None]])
    masks = jnp.repeat(masks, TILE, axis=2)
    kids, low, up = exchange(children, lower_panel, upper_panel, n_row, n_col, pc)
    return build_front(masks, kids, low, up, pr, pc)


def solution(mesh):
    placed = (P("row", "col"), P(), P(), P(), P("row", "col"), P("row", "col"))
    return jax.shard_map(
        body, mesh=mesh, in_specs=placed, out_specs=P("row", "col"), check_vma=False
    )
```

```python
import functools

import jax
import jax.numpy as jnp
from jax import lax
from jax.experimental import pallas as pl
from jax.experimental.pallas import tpu as pltpu
from jax.sharding import PartitionSpec as P

TILE = 128
WINDOW = 3
MESH = pl.DeviceIdType.MESH


def lanes(index):
    return pl.ds(pl.multiple_of(index * TILE, TILE), TILE)


def exchange_kernel(
    nx, nq, kc, pc,
    kids, low, up,
    recv, low_all, up_all,
    send1, recv1, send2, recv2, send3, recv3,
    up_s1, up_r1, up_s3, up_r3,
    low_sr, low_sl, low_sp, low_r,
):
    row = lax.axis_index("row")
    col = lax.axis_index("col")
    x, core = row // 2, row % 2
    q, p = col // 2, col % 2
    core_mate = (2 * x + 1 - core, col)
    p_mate = (row, 2 * q + 1 - p)

    barrier = pltpu.get_barrier_semaphore()
    for dx in range(nx):
        for dq in range(nq):
            if dx == 0 and dq == 0:
                continue
            pl.semaphore_signal(
                barrier, inc=1,
                device_id=(2 * lax.rem(x + dx, nx) + core, 2 * lax.rem(q + dq, nq) + p),
                device_id_type=MESH,
            )
    pl.semaphore_signal(barrier, inc=1, device_id=core_mate, device_id_type=MESH)
    pl.semaphore_signal(barrier, inc=1, device_id=p_mate, device_id_type=MESH)
    pl.semaphore_wait(barrier, nx * nq + 1)

    def remote(src, dst, ssem, rsem, device):
        return pltpu.make_async_remote_copy(
            src_ref=src, dst_ref=dst, send_sem=ssem, recv_sem=rsem,
            device_id=device, device_id_type=MESH,
        )

    def column_of(step, source_q):
        return lax.rem(step + source_q, kc)

    def unit1(step, tx):
        kk = column_of(step, q)
        j = col * kc + kk
        tq, s = j % nq, j // nq
        src = kids.at[:, tx, :, lanes(kk)]
        dst = recv.at[row, :, :, lanes(s)]
        here = (tx == x) & (tq == q)

        def far():
            device = (2 * tx + core, 2 * tq + p)
            return remote(src, dst, send1.at[kk, tx], recv1.at[x, s], device)

        def near():
            return pltpu.make_async_copy(src, dst, recv1.at[x, s])

        return here, far, near

    def issue(step):
        def one(dx, carry):
            here, far, near = unit1(step, lax.rem(x + 1 + dx, nx))

            @pl.when(here)
            def _():
                near().start()

            @pl.when(jnp.logical_not(here))
            def _():
                far().start()

            return carry

        lax.fori_loop(0, nx, one, 0)

    def drain(step):
        def one(dx, carry):
            here, far, _ = unit1(step, lax.rem(x + 1 + dx, nx))

            @pl.when(jnp.logical_not(here))
            def _():
                far().wait_send()

            return carry

        lax.fori_loop(0, nx, one, 0)

    def slot(xs, s, c):
        return recv.at[2 * xs + c, :, :, lanes(s)]

    def pair_copy(xs, s):
        ref = slot(xs, s, core)
        return remote(ref, ref, send2.at[xs, s], recv2.at[xs, s], p_mate)

    def core_copy(xs, s):
        ref = slot(xs, s, core)
        return remote(ref, ref, send3.at[xs, s], recv3.at[xs, s], core_mate)

    def arrivals(step, side, handle):
        def by_q(dq, carry):
            qs = lax.rem(q + dq, nq)
            j = (2 * qs + side) * kc + column_of(step, qs)

            @pl.when(j % nq == q)
            def _():
                lax.fori_loop(0, nx, lambda xs, c: (handle(xs, j // nq), c)[1], 0)

            return carry

        lax.fori_loop(0, nq, by_q, 0)

    def from_source(xs, s):
        ref = slot(xs, s, core)
        pltpu.make_async_copy(ref, ref, recv1.at[xs, s]).wait()
        pair_copy(xs, s).start()
        core_copy(xs, s).start()

    def from_pair(xs, s):
        pair_copy(xs, s).wait_recv()
        core_copy(xs, s).start()

    def up_far(tx):
        return remote(up, up_all.at[row], up_s1.at[tx], up_r1.at[x], (2 * tx + core, col))

    def up_core(xs):
        ref = up_all.at[2 * xs + core]
        return remote(ref, ref, up_s3.at[xs], up_r3.at[xs], core_mate)

    def low_slot(qs, owner):
        if len(low_all.shape) == 3:
            return low_all.at[2 * qs + owner]
        return low_all.at[:, lanes(2 * qs + owner)]

    def low_copy(qs, owner, sems, device):
        ref = low_slot(qs, owner)
        k = 2 * qs + owner
        return remote(ref, ref, sems.at[k], low_r.at[k], device)

    def low_right(qs, owner):
        return low_copy(qs, owner, low_sr, (row, 2 * (q + 1) + p))

    def low_left(qs, owner):
        return low_copy(qs, owner, low_sl, (row, 2 * (q - 1) + p))

    def low_pair(qs, owner):
        return low_copy(qs, owner, low_sp, p_mate)

    def goes_right(qs, owner):
        return (qs <= q) & (q + 1 < nq) & ((p == 0) | (owner == 1))

    def goes_left(qs, owner):
        return (qs >= q) & (q > 0) & ((p == 1) | (owner == 0))

    def goes_pair(qs, owner):
        return (owner == p) & ((qs == q) | ((qs < q) & (p == 0)) | ((qs > q) & (p == 1)))

    def from_pair_only(qs, owner):
        return (owner != p) & (qs != q) & jnp.logical_not(((qs < q) & (p == 0)) | ((qs > q) & (p == 1)))

    def low_wait(qs, owner):
        ref = low_slot(qs, owner)
        pltpu.make_async_copy(ref, ref, low_r.at[2 * qs + owner]).wait()

    def low_arrived(qs, owner):
        @pl.when(jnp.logical_not(from_pair_only(qs, owner)))
        def _():
            low_wait(qs, owner)

            @pl.when(goes_pair(qs, owner))
            def _():
                low_pair(qs, owner).start()

            @pl.when(goes_right(qs, owner))
            def _():
                low_right(qs, owner).start()

            @pl.when(goes_left(qs, owner))
            def _():
                low_left(qs, owner).start()

    def up_arrived(xs):
        ref = up_all.at[2 * xs + core]
        pltpu.make_async_copy(ref, ref, up_r1.at[xs]).wait()
        up_core(xs).start()

    pltpu.make_async_copy(low, low_slot(q, p), low_r.at[col]).start()
    pltpu.make_async_copy(up, up_all.at[row], up_r1.at[x]).start()
    for dx in range(1, nx):
        up_far(lax.rem(x + dx, nx)).start()
    for step in range(min(WINDOW, kc)):
        issue(step)

    def main(m, carry):
        @pl.when(m < nx)
        def _():
            up_arrived(lax.rem(x + m, nx))

        @pl.when((m < nq) & (q - m >= 0))
        def _():
            low_arrived(q - m, p)
            low_arrived(q - m, 1 - p)

        @pl.when((m > 0) & (q + m < nq))
        def _():
            low_arrived(q + m, p)
            low_arrived(q + m, 1 - p)

        @pl.when(m < kc)
        def _():
            drain(m)

            @pl.when(m + WINDOW < kc)
            def _():
                issue(m + WINDOW)

            arrivals(m, p, from_source)

        @pl.when((m >= 1) & (m < kc + 1))
        def _():
            arrivals(m - 1, 1 - p, from_pair)

        return carry

    lax.fori_loop(0, max(kc + 1, nq, nx), main, 0)

    def finish_x(xs, carry):
        up_core(xs).wait()

        @pl.when(xs != x)
        def _():
            up_far(xs).wait_send()

        def finish_s(s, inner):
            j = s * nq + q

            @pl.when((j // kc) % 2 == p)
            def _():
                pair_copy(xs, s).wait_send()

            core_copy(xs, s).wait()
            return inner

        lax.fori_loop(0, pc, finish_s, 0)
        return carry

    lax.fori_loop(0, nx, finish_x, 0)

    def finish_low(k, carry):
        qs, owner = k // 2, k % 2

        @pl.when(from_pair_only(qs, owner))
        def _():
            low_wait(qs, owner)

        @pl.when(goes_pair(qs, owner))
        def _():
            low_pair(qs, owner).wait_send()

        @pl.when(goes_right(qs, owner))
        def _():
            low_right(qs, owner).wait_send()

        @pl.when(goes_left(qs, owner))
        def _():
            low_left(qs, owner).wait_send()

        return carry

    lax.fori_loop(0, 2 * nq, finish_low, 0)


def exchange(children, lower_panel, upper_panel, n_row, n_col, pc):
    nx, nq = n_row // 2, n_col // 2
    rows, cols = children.shape
    kc = cols // TILE
    tk = rows // TILE // nx
    kids = children.reshape(tk, nx, TILE, cols)
    low_rows, low_cols = lower_panel.shape
    if low_cols == TILE:
        low_shape = (low_rows, n_col * TILE)
    else:
        low_shape = (n_col, low_rows, low_cols)
    dma = pltpu.SemaphoreType.DMA
    anywhere = pl.BlockSpec(memory_space=pl.ANY)
    recv, low_all, up_all = pl.pallas_call(
        functools.partial(exchange_kernel, nx, nq, kc, pc),
        out_shape=[
            jax.ShapeDtypeStruct((n_row, tk, TILE, pc * TILE), children.dtype),
            jax.ShapeDtypeStruct(low_shape, lower_panel.dtype),
            jax.ShapeDtypeStruct((n_row,) + upper_panel.shape, upper_panel.dtype),
        ],
        in_specs=[anywhere] * 3,
        out_specs=[anywhere] * 3,
        scratch_shapes=[
            dma((kc, nx)), dma((nx, pc)), dma((nx, pc)), dma((nx, pc)), dma((nx, pc)), dma((nx, pc)),
            dma((nx,)), dma((nx,)), dma((nx,)), dma((nx,)),
            dma((n_col,)), dma((n_col,)), dma((n_col,)), dma((n_col,)),
        ],
        compiler_params=pltpu.CompilerParams(
            collective_id=0, has_side_effects=True, vmem_limit_bytes=60 * 1024 * 1024
        ),
    )(kids, lower_panel, upper_panel)
    if low_cols != TILE:
        low_all = low_all.transpose(1, 0, 2).reshape(low_rows, n_col * low_cols)
    return (
        recv.reshape(2, n_row * tk * TILE // 2, pc * TILE),
        low_all,
        up_all.reshape(-1, pc * TILE),
    )


def front_kernel(band, width, masks, kids, low, up, out):
    first = pl.program_id(0) * band
    for start in range(0, out.shape[1], width):
        cols = pl.ds(start, width)
        product = jnp.dot(low[...], up[:, cols], preferred_element_type=jnp.float32)
        for k in range(band):
            rows = pl.ds(k * TILE, TILE)
            total = kids[0, rows, cols].astype(jnp.float32) * masks[0, pl.ds(first + k, 1), cols]
            total += kids[1, rows, cols].astype(jnp.float32) * masks[1, pl.ds(first + k, 1), cols]
            total -= product[k * TILE:(k + 1) * TILE] * masks[2, pl.ds(first + k, 1), cols]
            out[rows, cols] = total


def build_front(masks, kids, low, up, pr, pc):
    band = next(b for b in (4, 2, 1) if pr % b == 0)
    ncols, depth = pc * TILE, low.shape[1]
    width = next(w for w in (1280, 640, 512, 256, 128) if ncols % w == 0)
    return pl.pallas_call(
        functools.partial(front_kernel, band, width),
        grid=(pr // band,),
        out_shape=jax.ShapeDtypeStruct((pr * TILE, ncols), jnp.float32),
        in_specs=[
            pl.BlockSpec(memory_space=pltpu.VMEM),
            pl.BlockSpec((2, band * TILE, ncols), lambda i: (0, i, 0)),
            pl.BlockSpec((band * TILE, depth), lambda i: (i, 0)),
            pl.BlockSpec(memory_space=pltpu.VMEM),
        ],
        out_specs=pl.BlockSpec((band * TILE, ncols), lambda i: (i, 0)),
        compiler_params=pltpu.CompilerParams(vmem_limit_bytes=56 * 1024 * 1024),
        cost_estimate=pl.CostEstimate(
            flops=2 * pr * TILE * ncols * depth,
            bytes_accessed=8 * pr * TILE * ncols,
            transcendentals=0,
        ),
    )(masks, kids, low, up)


def body(children, row_maps, col_maps, pairs, lower_panel, upper_panel):
    n_row, n_col = lax.axis_size("row"), lax.axis_size("col")
    row, col = lax.axis_index("row"), lax.axis_index("col")
    nx, nq = n_row // 2, n_col // 2
    pr = lower_panel.shape[0] // TILE
    pc = upper_panel.shape[1] // TILE
    row_ids = row * pr + jnp.arange(pr, dtype=jnp.int32)
    col_ids = col * pc + jnp.arange(pc, dtype=jnp.int32)
    mine_rows = lax.dynamic_index_in_dim(row_maps.reshape(2, pr, nx), row // 2, 2, keepdims=False)
    mine_cols = lax.dynamic_index_in_dim(col_maps.reshape(2, pc, nq), col // 2, 2, keepdims=False)
    row_on = (mine_rows == row_ids[None]).astype(jnp.float32)
    col_on = (mine_cols == col_ids[None]).astype(jnp.float32)
    row_hit = (pairs[:, 0][:, None] == row_ids[None]).astype(jnp.bfloat16)
    col_hit = (pairs[:, 1][:, None] == col_ids[None]).astype(jnp.bfloat16)
    listed = jnp.dot(row_hit.T, col_hit, preferred_element_type=jnp.float32)
    masks = jnp.concatenate([row_on[:, :, None] * col_on[:, None, :], listed[None]])
    masks = jnp.repeat(masks, TILE, axis=2)
    kids, low, up = exchange(children, lower_panel, upper_panel, n_row, n_col, pc)
    return build_front(masks, kids, low, up, pr, pc)


def solution(mesh):
    placed = (P("row", "col"), P(), P(), P(), P("row", "col"), P("row", "col"))
    return jax.shard_map(
        body, mesh=mesh, in_specs=placed, out_specs=P("row", "col"), check_vma=False
    )
```
